512 devices in a mesh: section: 8 (over y_lo, core), dp: 64 (over y_hi, x, z).
Axes of the slice: x: 4, y: 8 (y_hi: 2, y_lo: 4; y = y_hi * 4 + y_lo), z: 8, core: 2. Of those that a mesh axis runs over, the one named last changes fastest.
Arguments:
- acts: bfloat16 [8, 64, 1, 64, 2, 2, 128], P('section', 'dp'), may hold values from -6 to 6
- preacts: bfloat16 [8, 64, 1, 64, 2, 2, 128], P('section', 'dp'), may hold values from -6 to 6
- top_grad: bfloat16 [64, 1, 64, 2, 2, 128], P('dp'), may hold values from -6 to 6
- weights: bfloat16 [8, 64, 1728], P('section'), may hold values from -0.21875 to 0.21875
- a_factor: bfloat16 [8, 1728, 1728], P('section', 'dp'), as said below
- g_factor: bfloat16 [8, 64, 64], P('section'), as said below
Outputs:
- act_grads: bfloat16 [8, 64, 1, 64, 2, 2, 128], P('section', 'dp')
- update: float32 [8, 1728, 64], P('section', 'dp')
- inverse: float32 [8, 1728, 1728], P('section', 'dp')
The draws below stay inside these ranges and needn't reach their ends.
Inputs may be any that keep to these rules, and one draw needn't show every extreme that they name: `a_factor`: each matrix is symmetric and positive definite. `g_factor`: each matrix is symmetric and positive definite.
All inputs are finite; a program needn't handle non-finite values. Where the reference program divides by a largest or mean magnitude, that divisor is 1e-20 or more.
Results may differ from the reference program's by a relative error of at most 0.006.
Values may be sent and summed in bfloat16 or wider, within the bound.
A program may use at most 64 MiB of HBM per device.

```python
import math
import jax
import jax.numpy as jnp
from jax import lax

C = 64
KW = 3
VX = 2
VY = 2
VZ = 128
MICRO = 1
TAPS = 27
OA = 1728
SECTIONS = 8
REPLICAS = 64
N_SECTION = 8
N_DP = 64


def spd_matrices(key, count, order_full):
    key_perm, key_noise, key_scale = jax.random.split(key, 3)
    decay = 0.9
    orders = jax.vmap(lambda one_key: jax.random.permutation(one_key, order_full))(jax.random.split(key_perm, count))
    distance = jnp.abs(orders[:, :, None] - orders[:, None, :]).astype(jnp.float32)
    kernel = jnp.exp(distance * math.log(decay))
    integers = jax.random.randint(key_noise, (count, order_full, order_full), -2, 3).astype(jnp.float32)
    wishart = jnp.einsum('cik,cjk->cij', integers, integers, precision=lax.Precision.HIGHEST) / (2.0 * order_full)
    identity = jnp.eye(order_full, dtype=jnp.float32)
    base_matrix = kernel + 0.1 * wishart + 0.05 * identity[None]
    ramp_up = 1.0 + 2.0 * jnp.arange(order_full, dtype=jnp.float32) / max(order_full - 1, 1)
    spread = jax.random.uniform(key_scale, (count, order_full), jnp.float32, 0.5, 1.5)
    scales = ramp_up[None, :] * spread
    root_scale = jnp.sqrt(scales)
    return base_matrix * root_scale[:, :, None] * root_scale[:, None, :]


def draw_a_factor(key, part):
    return spd_matrices(jax.random.fold_in(key, 11), SECTIONS, OA).astype(jnp.bfloat16)


def draw_g_factor(key, part):
    return spd_matrices(jax.random.fold_in(key, 23), SECTIONS, C).astype(jnp.bfloat16)


def shard_levels(own_key, dims, shards, smallest, top_value):
    def one(position, shards_of):
        draws = jax.random.uniform(jax.random.fold_in(jax.random.fold_in(own_key, 6), position), (shards_of,), jnp.float32, smallest / len(shards), top_value / len(shards))
        return jnp.repeat(jnp.exp(draws), dims[position] // shards_of).reshape((-1,) + (1,) * (len(dims) - position - 1))

    factor_of = one(*shards[0])
    for cut in shards[1:]:
        factor_of = factor_of * one(*cut)
    return factor_of


def scatter_about(key, dims, scale, bound, cuts=(), kind=jnp.bfloat16):
    entries = scale * jax.random.normal(key, dims, jnp.float32)
    if cuts:
        entries = entries * shard_levels(key, dims, cuts, -0.22, 0.18)
    return jnp.clip(entries, -bound, bound).astype(kind)


def setup_inputs(seed: int = 0) -> dict:
    key_of = jax.random.split(jax.random.key(seed), 7)
    return {
        "acts": scatter_about(key_of[0], (SECTIONS, REPLICAS, MICRO, C, VX, VY, VZ), 1.0, 6.0, ((0, 8), (1, 64))),
        "preacts": scatter_about(key_of[1], (SECTIONS, REPLICAS, MICRO, C, VX, VY, VZ), 1.0, 6.0, ((0, 8), (1, 64))),
        "top_grad": scatter_about(key_of[2], (REPLICAS, MICRO, C, VX, VY, VZ), 1.0, 6.0, ((0, 64),)),
        "weights": scatter_about(key_of[3], (SECTIONS, C, OA), (TAPS * C // 2) ** -0.5, 0.21875, ((0, 8),)),
        "a_factor": draw_a_factor(jax.random.fold_in(key_of[6], 71), 0),
        "g_factor": draw_g_factor(jax.random.fold_in(key_of[6], 71), 0),
    }


def tap_offsets(kernel_width):
    middle = kernel_width // 2
    result = []
    for along_x in range(kernel_width):
        for along_y in range(kernel_width):
            for along_z in range(kernel_width):
                result.append((along_x - middle, along_y - middle, along_z - middle))
    return result


def taps_stack(volume, kernel_width, direction):
    middle = kernel_width // 2
    padded = jnp.pad(volume, ((0, 0), (middle, middle), (middle, middle), (middle, middle)))
    size_x, size_y, size_z = volume.shape[1], volume.shape[2], volume.shape[3]
    pieces = []
    for off_x, off_y, off_z in tap_offsets(kernel_width):
        start_x = middle + direction * off_x
        start_y = middle + direction * off_y
        start_z = middle + direction * off_z
        pieces.append(padded[:, start_x:start_x + size_x, start_y:start_y + size_y, start_z:start_z + size_z])
    stacked = jnp.stack(pieces, 0)
    return stacked.reshape(len(pieces) * volume.shape[0], size_x * size_y * size_z)


def back_input(grad_out, w_rows):
    columns = taps_stack(grad_out, KW, -1)
    summed = lax.dot_general(w_rows.astype(jnp.float32), columns.astype(jnp.float32), (((0,), (0,)), ((), ())))
    return summed.astype(jnp.bfloat16).reshape(grad_out.shape)


def back_weight(volume, grad_out):
    columns = taps_stack(volume, KW, 1)
    flattened = grad_out.reshape(grad_out.shape[0], -1)
    return lax.dot_general(columns.astype(jnp.float32), flattened.astype(jnp.float32), (((1,), (1,)), ((), ())))


def newton_inverse(matrix):
    values = matrix.astype(jnp.float32)
    step_size = 1.0 / jnp.max(jnp.sum(jnp.abs(values), axis=1))
    identity = jnp.eye(matrix.shape[0], dtype=jnp.float32)
    resid0 = (identity - step_size * values).astype(jnp.bfloat16)
    resid1 = jnp.dot(resid0.astype(jnp.float32), resid0.astype(jnp.float32)).astype(jnp.bfloat16)
    cross_term = jnp.dot(resid1.astype(jnp.float32), resid0.astype(jnp.float32))
    return step_size * (identity + resid0.astype(jnp.float32) + resid1.astype(jnp.float32) + cross_term)


def reference(acts, preacts, top_grad, weights, a_factor, g_factor):
    section_grads = [None] * N_SECTION
    updates = [None] * N_SECTION
    inverses = [None] * N_SECTION
    for section_now in reversed(range(N_SECTION)):
        w_rows = weights[section_now].reshape(C, TAPS, C).transpose(1, 0, 2).reshape(TAPS * C, C)
        if section_now == N_SECTION - 1:
            arriving_all = top_grad
        else:
            arriving_all = section_grads[section_now + 1]

        def replica_pass(operands):
            inputs, pre_values, arriving = operands
            sent = []
            grad_sum = jnp.zeros((OA, C), jnp.float32)
            for micro in range(MICRO):
                grad_out = jnp.where(pre_values[micro] > 0, arriving[micro], jnp.zeros_like(arriving[micro]))
                sent.append(back_input(grad_out, w_rows))
                grad_sum = grad_sum + back_weight(inputs[micro], grad_out)
            return jnp.stack(sent, 0), grad_sum

        sent_all, local_grads = lax.map(replica_pass, (acts[section_now], preacts[section_now], arriving_all))
        section_grads[section_now] = sent_all
        mean_grad = jnp.sum(local_grads, axis=0) / N_DP
        inverse_now = newton_inverse(a_factor[section_now])
        g_inverse = newton_inverse(g_factor[section_now])
        preconditioned = jnp.dot(mean_grad, g_inverse, precision=lax.Precision.HIGHEST, preferred_element_type=jnp.float32)
        updates[section_now] = jnp.dot(inverse_now, preconditioned, precision=lax.Precision.HIGHEST, preferred_element_type=jnp.float32)
        inverses[section_now] = inverse_now
    return jnp.stack(section_grads, 0), jnp.stack(updates, 0), jnp.stack(inverses, 0)
```

```python
import functools

import jax
import jax.numpy as jnp
from jax import lax
from jax.experimental import pallas as pl
from jax.experimental.pallas import tpu as pltpu
from jax.sharding import PartitionSpec as P

MESH = pl.DeviceIdType.MESH
F32 = jnp.float32
BF16 = jnp.bfloat16
HIGH = lax.Precision.HIGHEST

ORDER = 1728
PAIRED = [((a, 2, c), (a, 0, c)) for a in range(3) for c in range(3)]
MIDDLE = [(a, 1, c) for a in range(3) for c in range(3)]
PAIRED += [(MIDDLE[2 * m], MIDDLE[min(2 * m + 1, 8)]) for m in range(5)]
TILES = len(PAIRED)


def tap_of(abc):
    return (abc[0] * 3 + abc[1]) * 3 + abc[2]


def iota(shape, dim):
    return lax.broadcasted_iota(jnp.int32, shape, dim)


def ones_where(mask):
    return jnp.where(mask, 1.0, 0.0).astype(BF16)


def mm(left, right, precision=None):
    return lax.dot_general(
        left, right, (((1,), (0,)), ((), ())), precision=precision, preferred_element_type=F32
    )


def mm_nt(left, right):
    return lax.dot_general(left, right, (((1,), (1,)), ((), ())), preferred_element_type=F32)


def pad_to(value, step):
    return -(-value // step) * step


def kernel(cfg, acts, pre, top, w, a, gf, og, ou, oi, *scratch):
    (
        wt, bw, pre_p, top_p, ash, arr, obuf, gcat, own, apad, sel, piece, spc, mx,
        rcol32, rcol, pbuf, prc, xf, xcat, wg, rg, sbuf, rs, pch, pag, pall,
        gbd,
        ch_s, ch_r, fa_s, fa_r, sa_s, sa_r, sm_s, sm_r, pr_s, pr_r,
        gr_s, gr_r, rr_s, rr_r, as_s, as_r, af_s, af_r,
    ) = scratch
    n_sec, nf, ns, rows, rpad, early = cfg
    blk = rows * nf
    cw = sel.shape[1]
    frows = rg.shape[1]
    srows = rs.shape[1]
    sec = lax.axis_index("section")
    dp = lax.axis_index("dp")
    fi = lax.rem(dp, nf)
    si = dp // nf

    def f_peer(k):
        return lax.rem(fi + k, nf)

    def f_from(k):
        return lax.rem(fi - k + nf, nf)

    def s_peer(k):
        return lax.rem(si + k, ns)

    def s_from(k):
        return lax.rem(si - k + ns, ns)

    def f_dev(index):
        return (sec, si * nf + index)

    def s_dev(index):
        return (sec, index * nf + fi)

    def copy_to(src, dst, ss, rr, k, device):
        return pltpu.make_async_remote_copy(
            src_ref=src, dst_ref=dst, send_sem=ss.at[k - 1], recv_sem=rr.at[k - 1],
            device_id=device, device_id_type=MESH,
        )

    def each(count, body):
        lax.fori_loop(1, count, lambda k, carry: (body(k), carry)[1], 0)

    barrier = pltpu.get_barrier_semaphore()
    each(nf, lambda k: pl.semaphore_signal(barrier, inc=1, device_id=f_dev(f_peer(k)), device_id_type=MESH))
    each(ns, lambda k: pl.semaphore_signal(barrier, inc=1, device_id=s_dev(s_peer(k)), device_id_type=MESH))

    for near in (sec + 1, sec + n_sec - 1):
        pl.semaphore_signal(
            barrier, inc=1, device_id=(lax.rem(near, n_sec), dp), device_id_type=MESH
        )

    own[...] = jnp.zeros_like(own)
    own[0:rows, :] = a[...]
    pl.semaphore_wait(barrier, nf + ns)

    def fa_copy(k, slot, index):
        return copy_to(own, apad.at[slot], fa_s, fa_r, k, f_dev(index))

    each(nf, lambda k: fa_copy(k, fi, f_peer(k)).start())
    apad[fi] = own[...]

    wpair = jnp.concatenate([w[...], w[...]], axis=0).astype(F32)
    for m in range(ORDER // 128):
        wt[128 * m : 128 * m + 128, :] = wpair[:, 128 * m : 128 * m + 128].T
    last = 128 * (ORDER // 128)
    wt[last:ORDER, :] = wpair[:, last:ORDER].T
    left64 = iota((64, 128), 1) < 64

    def wtap(aa, b, c):
        start = 64 * tap_of((aa, b, c))
        return wt[start : start + 64, :]

    for c in range(3):
        for x in range(2):
            for y in range(2):
                for x2 in range(2):
                    block = jnp.where(left64, wtap(x - x2 + 1, y + 1, c), wtap(x - x2 + 1, y, c))
                    row = 64 * (2 * x + y)
                    lane = 256 * c + 128 * x2
                    bw[row : row + 64, lane : lane + 128] = block.astype(BF16)

    out_row, in_row = (iota((256, 256), 0), iota((256, 256), 1))
    perm = ones_where(in_row == (out_row & 63) * 4 + (out_row >> 6))
    pre_p[...] = mm(perm, pre[...])
    top_p[...] = mm(perm, top[...])
    lanes = iota((256, 128), 1)
    act_p = mm(perm, acts[...])
    ash[0:256, :] = jnp.where(lanes == 0, 0.0, pltpu.roll(act_p, 1, 1)).astype(BF16)
    ash[256:512, :] = act_p.astype(BF16)
    ash[512:768, :] = jnp.where(lanes == 127, 0.0, pltpu.roll(act_p, 127, 1)).astype(BF16)

    def send_chain():
        return pltpu.make_async_remote_copy(
            src_ref=obuf, dst_ref=arr, send_sem=ch_s, recv_sem=ch_r,
            device_id=(lax.rem(sec - 1 + n_sec, n_sec), dp), device_id_type=MESH,
        )

    def gr_copy(k, chunk, slot):
        return copy_to(
            wg.at[pl.ds(pl.multiple_of(chunk * frows, frows), frows), :], rg.at[slot],
            gr_s, gr_r, k, f_dev(chunk),
        )

    def holds(chunk):
        return chunk * frows < TILES * 64

    def relay():
        @pl.when(sec < n_sec - 1)
        def _():
            send_chain().wait_recv()
            top_p[...] = arr[...].astype(F32)

        lane = iota((256, 128), 1)
        grad = jnp.where(pre_p[...] > 0, top_p[...], 0.0)
        gcat[256:512, :] = grad.astype(BF16)
        gcat[0:256, :] = jnp.where(lane == 127, 0.0, pltpu.roll(grad, 127, 1)).astype(BF16)
        gcat[512:768, :] = jnp.where(lane == 0, 0.0, pltpu.roll(grad, 1, 1)).astype(BF16)
        obuf[...] = mm(bw[...], gcat[...]).astype(BF16)

        @pl.when(sec > 0)
        def _():
            send_chain().start()

        back_row, back_col = (iota((256, 256), 0), iota((256, 256), 1))
        back = ones_where(back_row == (back_col & 63) * 4 + (back_col >> 6))
        og[...] = mm(back, obuf[...]).astype(BF16)

        full = mm_nt(ash[...], gcat[256:512, :])
        left = iota((64, 128), 1) < 64

        def part(aa, c, y):
            total = None
            for x in range(2):
                x2 = x - (aa - 1)
                if 0 <= x2 < 2:
                    row = 256 * c + 64 * (2 * x + y)
                    term = full[row : row + 64, 128 * x2 : 128 * x2 + 128]
                    total = term if total is None else total + term
            return total

        parts = {(aa, c, y): part(aa, c, y) for aa in range(3) for c in range(3) for y in range(2)}
        for m, (one, two) in enumerate(PAIRED):
            if one[1] == 2:
                tile = jnp.where(left, parts[one[0], one[2], 1], parts[one[0], one[2], 0])
            else:
                first = parts[one[0], one[2], 0] + pltpu.roll(parts[one[0], one[2], 1], 64, 1)
                second = pltpu.roll(parts[two[0], two[2], 0], 64, 1) + parts[two[0], two[2], 1]
                tile = jnp.where(left, first, second)
            wg[64 * m : 64 * m + 64, :] = tile.astype(wg.dtype)

        def start(k):
            @pl.when(holds(f_peer(k)))
            def _():
                gr_copy(k, f_peer(k), fi).start()

        each(nf, start)

    if wg.shape[0] > 64 * TILES:
        wg[64 * TILES :, :] = jnp.zeros((wg.shape[0] - 64 * TILES, 128), wg.dtype)

    @pl.when(sec >= early)
    def _():
        relay()

    dup = ones_where(iota((64, 128), 0) == (iota((64, 128), 1) & 63))
    dup_t = ones_where(iota((128, 64), 1) == (iota((128, 64), 0) & 63))
    wide = mm(mm(dup_t, gf[...]).astype(BF16), dup)
    g_row, g_col = (iota((128, 128), 0), iota((128, 128), 1))
    values = jnp.where((g_row >> 6) == (g_col >> 6), wide, 0.0)
    g_step = 1.0 / jnp.max(jnp.sum(jnp.abs(values), axis=1, keepdims=True), axis=0, keepdims=True)
    g_eye = jnp.where(g_row == g_col, 1.0, 0.0)
    g_res0 = (g_eye - g_step * values).astype(BF16)
    g_res1 = mm(g_res0, g_res0).astype(BF16)
    gbd[...] = g_step * (g_eye + g_res0.astype(F32) + g_res1.astype(F32) + mm(g_res1, g_res0))

    sel[...] = ones_where((iota((ORDER, cw), 0) == fi * blk + iota((ORDER, cw), 1)) & (iota((ORDER, cw), 1) < blk))

    each(nf, lambda k: fa_copy(k, f_from(k), f_peer(k)).wait_recv())
    rows_all = apad[...].reshape(nf * rpad, ORDER)
    row_sums = jnp.sum(jnp.abs(rows_all.astype(F32)), axis=1, keepdims=True)
    piece[...] = mm(rows_all, sel[...]).astype(BF16)
    mx[si] = jnp.broadcast_to(jnp.max(row_sums, axis=0, keepdims=True), (8, 128))

    def sa_copy(k, slot, index):
        return copy_to(piece, spc.at[slot], sa_s, sa_r, k, s_dev(index))

    def sm_copy(k, slot, index):
        return copy_to(mx.at[si], mx.at[slot], sm_s, sm_r, k, s_dev(index))

    each(ns, lambda k: sm_copy(k, si, s_peer(k)).start())
    each(ns, lambda k: sa_copy(k, si, s_peer(k)).start())
    spc[si] = piece[...]
    each(ns, lambda k: sm_copy(k, s_from(k), s_peer(k)).wait_recv())
    each(ns, lambda k: sa_copy(k, s_from(k), s_peer(k)).wait_recv())
    largest = jnp.max(jnp.max(mx[...], axis=0), axis=0, keepdims=True)[:, 0:1]
    step = 1.0 / largest

    squeeze_row, squeeze_col = (iota((blk, nf * rpad), 0), iota((blk, nf * rpad), 1))
    in_slot = lax.rem(squeeze_col, rpad)
    squeeze = ones_where(((squeeze_col // rpad) * rows + in_slot == squeeze_row) & (in_slot < rows))
    for h in range(ns):
        rcol32[h * blk : h * blk + blk, :] = mm(squeeze, spc[h])
    col_row, col_col = (iota((ORDER, cw), 0), iota((ORDER, cw), 1))
    col_eye = jnp.where((col_row == fi * blk + col_col) & (col_col < blk), 1.0, 0.0)
    rcol[...] = (col_eye - step * rcol32[...]).astype(BF16)

    local = iota((nf * rpad, ORDER), 0)
    slot_row = lax.rem(local, rpad)
    row_eye = jnp.where(
        (iota((nf * rpad, ORDER), 1) == si * blk + (local // rpad) * rows + slot_row) & (slot_row < rows), 1.0, 0.0
    )
    rrow = (row_eye - step * apad[...].reshape(nf * rpad, ORDER).astype(F32)).astype(BF16)
    square = mm(rrow, rcol[...]).astype(BF16)
    partial = mm_nt(square, rcol[...]) + mm_nt(square, sel[...])
    pbuf[...] = partial.astype(BF16).reshape(pbuf.shape)

    def pr_copy(k, chunk, slot):
        return copy_to(pbuf.at[chunk], prc.at[slot], pr_s, pr_r, k, f_dev(chunk))

    each(nf, lambda k: pr_copy(k, f_peer(k), fi).start())
    prc[fi] = pbuf[fi]
    each(nf, lambda k: pr_copy(k, f_peer(k), f_from(k)).wait_recv())

    own_row = iota((rpad, ORDER), 0)
    own_eye = jnp.where((iota((rpad, ORDER), 1) == dp * rows + own_row) & (own_row < rows), 1.0, 0.0)
    own_res = (own_eye - step * own[...].astype(F32)).astype(BF16).astype(F32)
    summed = prc[0].astype(F32)
    for k in range(1, nf):
        summed = summed + prc[k].astype(F32)
    inverse = step * (own_eye + own_res + summed)
    oi[:, 0, :] = inverse[0:rows, :]

    xf[...] = jnp.zeros_like(xf)
    xf[:, 0:ORDER] = inverse
    left_x = iota((rpad, 128), 1) < 64

    def tap_lanes(abc, half):
        tap = tap_of(abc)
        group = xf[:, 128 * (tap // 2) : 128 * (tap // 2) + 128]
        return group if tap % 2 == half else pltpu.roll(group, 64, 1)

    for side in range(2):
        for m in range(TILES // 2):
            one, two = (PAIRED[2 * m][side], PAIRED[2 * m + 1][side])
            tile = jnp.where(left_x, tap_lanes(one, 0), tap_lanes(two, 1))
            if side == 1 and 2 * m + 1 == TILES - 1:
                tile = jnp.where(left_x, tile, 0.0)
            high = tile.astype(BF16)
            low = (tile - high.astype(F32)).astype(BF16)
            xcat[2 * side * rpad : 2 * side * rpad + rpad, 128 * m : 128 * m + 128] = high
            xcat[2 * side * rpad + rpad : 2 * side * rpad + 2 * rpad, 128 * m : 128 * m + 128] = low

    @pl.when(sec < early)
    def _():
        relay()

    @pl.when(holds(fi))
    def _():
        rg[fi] = wg[pl.ds(pl.multiple_of(fi * frows, frows), frows), :]
        each(nf, lambda k: gr_copy(k, fi, f_from(k)).wait_recv())
        total = rg[0].astype(F32)
        for k in range(1, nf):
            total = total + rg[k].astype(F32)
        sbuf[...] = total.reshape(sbuf.shape)

        def rr_copy(k, chunk, slot):
            return copy_to(sbuf.at[chunk], rs.at[slot], rr_s, rr_r, k, s_dev(chunk))

        each(ns, lambda k: rr_copy(k, s_peer(k), si).start())
        rs[si] = sbuf[si]
        each(ns, lambda k: rr_copy(k, s_peer(k), s_from(k)).wait_recv())
        grad_sum = rs[0]
        for k in range(1, ns):
            grad_sum = grad_sum + rs[k]
        mean = grad_sum / (nf * ns)
        pch[...] = mm(mean, gbd[...], HIGH).astype(BF16)

        def as_copy(k, slot, index):
            return copy_to(pch, pag.at[slot], as_s, as_r, k, s_dev(index))

        each(ns, lambda k: as_copy(k, si, s_peer(k)).start())
        pag[si] = pch[...]
        each(ns, lambda k: as_copy(k, s_from(k), s_peer(k)).wait_recv())
        pall[fi] = pag[...].reshape(frows, 128)
        each(ns, lambda k: rr_copy(k, s_peer(k), si).wait_send())
        each(ns, lambda k: as_copy(k, si, s_peer(k)).wait_send())

    def af_copy(k, slot, index):
        return copy_to(pall.at[fi], pall.at[slot], af_s, af_r, k, f_dev(index))

    @pl.when(holds(fi))
    def _():
        each(nf, lambda k: af_copy(k, fi, f_peer(k)).start())

    def af_wait(k):
        @pl.when(holds(f_from(k)))
        def _():
            af_copy(k, f_from(k), f_peer(k)).wait_recv()

    each(nf, af_wait)
    terms = mm(xcat[...], pall[...].reshape(nf * frows, 128)[0 : 64 * TILES, :])
    firsts = terms[0:rpad, :] + terms[rpad : 2 * rpad, :]
    seconds = terms[2 * rpad : 3 * rpad, :] + terms[3 * rpad : 4 * rpad, :]
    update = firsts + pltpu.roll(seconds, 64, 1)
    ou[:, 0, :] = update[0:rows, 0:64]

    each(nf, lambda k: fa_copy(k, fi, f_peer(k)).wait_send())
    each(ns, lambda k: sm_copy(k, si, s_peer(k)).wait_send())
    each(ns, lambda k: sa_copy(k, si, s_peer(k)).wait_send())
    each(nf, lambda k: pr_copy(k, f_peer(k), fi).wait_send())

    def gr_done(k):
        @pl.when(holds(f_peer(k)))
        def _():
            gr_copy(k, f_peer(k), fi).wait_send()

    each(nf, gr_done)

    @pl.when(holds(fi))
    def _():
        each(nf, lambda k: af_copy(k, fi, f_peer(k)).wait_send())

    @pl.when(sec > 0)
    def _():
        send_chain().wait_send()


def make_call(n_sec, nf, ns, grad_type=BF16, early=None):
    rows = ORDER // (nf * ns)
    rpad = pad_to(rows, 16)
    blk = rows * nf
    cw = pad_to(blk, 128)
    frows = 1024 // nf
    srows = frows // ns
    early = n_sec // 2 if early is None else early
    cfg = (n_sec, nf, ns, rows, rpad, early)
    vmem = pltpu.VMEM
    dma = pltpu.SemaphoreType.DMA
    scratch = [
        vmem((ORDER, 128), F32),
        vmem((256, 768), BF16),
        vmem((256, 128), F32),
        vmem((256, 128), F32),
        vmem((768, 128), BF16),
        vmem((256, 128), BF16),
        vmem((256, 128), BF16),
        vmem((768, 128), BF16),
        vmem((rpad, ORDER), BF16),
        vmem((nf, rpad, ORDER), BF16),
        vmem((ORDER, cw), BF16),
        vmem((nf * rpad, cw), BF16),
        vmem((ns, nf * rpad, cw), BF16),
        vmem((ns, 8, 128), F32),
        vmem((ORDER, cw), F32),
        vmem((ORDER, cw), BF16),
        vmem((nf, rpad, ORDER), BF16),
        vmem((nf, rpad, ORDER), BF16),
        vmem((rpad, pad_to(ORDER, 128)), F32),
        vmem((4 * rpad, 64 * TILES), BF16),
        vmem((1024, 128), grad_type),
        vmem((nf, frows, 128), grad_type),
        vmem((ns, srows, 128), F32),
        vmem((ns, srows, 128), F32),
        vmem((srows, 128), BF16),
        vmem((ns, srows, 128), BF16),
        vmem((nf, frows, 128), BF16),
        vmem((128, 128), F32),
        dma, dma,
    ]
    for count in (nf, ns, ns, nf, nf, ns, ns, nf):
        scratch += [dma((count - 1,)), dma((count - 1,))]
    spec = pl.BlockSpec(memory_space=pltpu.VMEM)
    return pl.pallas_call(
        functools.partial(kernel, cfg),
        out_shape=(
            jax.ShapeDtypeStruct((256, 128), BF16),
            jax.ShapeDtypeStruct((rows, 1, 64), F32),
            jax.ShapeDtypeStruct((rows, 1, ORDER), F32),
        ),
        in_specs=[spec] * 6,
        out_specs=(spec, spec, spec),
        scratch_shapes=scratch,
        compiler_params=pltpu.CompilerParams(
            collective_id=0, has_side_effects=True, vmem_limit_bytes=48 * 1024 * 1024
        ),
    )


def build(mesh, nf, ns, early=None):
    n_sec = mesh.shape["section"]

    def shards(acts, preacts, top_grad, weights, a_factor, g_factor):
        call = make_call(n_sec, nf, ns, early=early)
        grads, update, inverse = call(
            acts.reshape(256, 128),
            preacts.reshape(256, 128),
            top_grad.reshape(256, 128),
            weights[0],
            a_factor[0],
            g_factor[0],
        )
        return (
            grads.reshape(acts.shape),
            update.transpose(1, 0, 2),
            inverse.transpose(1, 0, 2),
        )

    placed = (
        P("section", "dp", None, None, None, None, None),
        P("section", "dp", None, None, None, None, None),
        P("dp", None, None, None, None, None),
        P("section", None, None),
        P("section", "dp", None),
        P("section", None, None),
    )
    return jax.shard_map(
        shards,
        mesh=mesh,
        in_specs=placed,
        out_specs=(
            P("section", "dp", None, None, None, None, None),
            P("section", "dp", None),
            P("section", "dp", None),
        ),
        check_vma=False,
    )


def solution(mesh):
    return build(mesh, 8, mesh.shape["dp"] // 8)
```

```python
import functools

import jax
import jax.numpy as jnp
from jax import lax
from jax.experimental import pallas as pl
from jax.experimental.pallas import tpu as pltpu
from jax.sharding import PartitionSpec as P

MESH = pl.DeviceIdType.MESH
F32 = jnp.float32
BF16 = jnp.bfloat16
HIGH = lax.Precision.HIGHEST

ORDER = 1728
PAIRED = [((a, 2, c), (a, 0, c)) for a in range(3) for c in range(3)]
MIDDLE = [(a, 1, c) for a in range(3) for c in range(3)]
PAIRED += [(MIDDLE[2 * m], MIDDLE[min(2 * m + 1, 8)]) for m in range(5)]
TILES = len(PAIRED)
PARTS = ("inv", "chain", "red")
EARLY = 2
VMEM_MIB = 56


def tap_of(abc):
    return (abc[0] * 3 + abc[1]) * 3 + abc[2]


def iota(shape, dim):
    return lax.broadcasted_iota(jnp.int32, shape, dim)


def ones_where(mask):
    return jnp.where(mask, 1.0, 0.0).astype(BF16)


def mm(left, right, precision=None):
    return lax.dot_general(
        left, right, (((1,), (0,)), ((), ())), precision=precision, preferred_element_type=F32
    )


def mm_nt(left, right):
    return lax.dot_general(left, right, (((1,), (1,)), ((), ())), preferred_element_type=F32)


def pad_to(value, step):
    return -(-value // step) * step


def kernel(cfg, acts_h, pre_h, top_h, w_h, a_h, gf_h, og, ou, oi, *scratch):
    (
        acts, pre, top, w, a, gf, in_s,
        wt, bw, pre_p, top_p, ash, arr, obuf, gcat, own, apad, sel, squeeze, spc, piece, mx,
        rrow, rcol, pbuf, prc, xf, xcat, wg, rg, sbuf, rs, pall, gbd, stp,
        ch_s, ch_r, fa_s, fa_r, sa_s, sa_r, sm_s, sm_r, pr_s, pr_r,
        gr_s, gr_r, rr_s, rr_r, af_s, af_r,
    ) = scratch
    n_sec, n, rows, rpad, early = cfg
    blk = rows * n
    cw = sel.shape[1]
    frows = rg.shape[1]
    sec = lax.axis_index("section")
    dp = lax.axis_index("dp")
    core = lax.rem(sec, 2)
    low, high = lax.rem(dp, n), dp // n
    fi = low + core * (high - low)
    si = high + core * (low - high)

    def f_dp(index):
        return si * n + index + core * (n - 1) * (index - si)

    def s_dp(index):
        return index * n + fi + core * (n - 1) * (fi - index)

    def f_peer(k):
        return lax.rem(fi + k, n)

    def f_from(k):
        return lax.rem(fi - k + n, n)

    def s_peer(k):
        return lax.rem(si + k, n)

    def s_from(k):
        return lax.rem(si - k + n, n)

    def f_dev(index):
        return (sec, f_dp(index))

    def s_dev(index):
        return (sec, s_dp(index))

    def copy_to(src, dst, ss, rr, k, device):
        return pltpu.make_async_remote_copy(
            src_ref=src, dst_ref=dst, send_sem=ss.at[k - 1], recv_sem=rr.at[k - 1],
            device_id=device, device_id_type=MESH,
        )

    def each(body):
        lax.fori_loop(1, n, lambda k, carry: (body(k), carry)[1], 0)

    def fa_copy(k, slot, index):
        return copy_to(own, apad.at[slot], fa_s, fa_r, k, f_dev(index))

    def sa_copy(k, slot, index, by_column):
        dst = spc.at[:, slot] if by_column else spc.at[slot]
        return copy_to(piece, dst, sa_s, sa_r, k, s_dev(index))

    def sm_copy(k, slot, index):
        return copy_to(mx.at[si], mx.at[slot], sm_s, sm_r, k, s_dev(index))

    def pr_copy(k, chunk, slot):
        return copy_to(pbuf.at[chunk], prc.at[slot], pr_s, pr_r, k, f_dev(chunk))

    def gr_copy(k, chunk, slot):
        return copy_to(wg.at[chunk], rg.at[slot], gr_s, gr_r, k, f_dev(chunk))

    def rr_copy(k, slot, index):
        return copy_to(sbuf, rs.at[slot], rr_s, rr_r, k, s_dev(index))

    def af_copy(k, slot, index):
        return copy_to(pall.at[fi], pall.at[slot], af_s, af_r, k, f_dev(index))

    def send_chain():
        return pltpu.make_async_remote_copy(
            src_ref=obuf, dst_ref=arr, send_sem=ch_s, recv_sem=ch_r,
            device_id=(lax.rem(sec - 1 + n_sec, n_sec), dp), device_id_type=MESH,
        )

    def holds(chunk):
        return chunk * frows < TILES * 64

    inputs = [
        pltpu.make_async_copy(src, dst, in_s.at[m])
        for m, (src, dst) in enumerate(
            [(a_h, a), (w_h, w), (pre_h, pre), (top_h, top), (acts_h, acts), (gf_h, gf)]
        )
    ]

    def conv_matrices():
        wpair = jnp.concatenate([w[...], w[...]], axis=0).astype(F32)
        for m in range(ORDER // 128):
            wt[128 * m : 128 * m + 128, :] = wpair[:, 128 * m : 128 * m + 128].T
        last = 128 * (ORDER // 128)
        wt[last:ORDER, :] = wpair[:, last:ORDER].T
        left64 = iota((64, 128), 1) < 64

        def wtap(aa, b, c):
            start = 64 * tap_of((aa, b, c))
            return wt[start : start + 64, :]

        for c in range(3):
            for x in range(2):
                for y in range(2):
                    for x2 in range(2):
                        block = jnp.where(left64, wtap(x - x2 + 1, y + 1, c), wtap(x - x2 + 1, y, c))
                        row = 64 * (2 * x + y)
                        lane = 256 * c + 128 * x2
                        bw[row : row + 64, lane : lane + 128] = block.astype(BF16)

    def channel_last(forward):
        one, two = (iota((256, 256), 0), iota((256, 256), 1))
        if not forward:
            one, two = two, one
        return ones_where(two == (one & 63) * 4 + (one >> 6))

    def small_inverse():
        dup = ones_where(iota((64, 128), 0) == (iota((64, 128), 1) & 63))
        dup_t = ones_where(iota((128, 64), 1) == (iota((128, 64), 0) & 63))
        wide = mm(mm(dup_t, gf[...]).astype(BF16), dup)
        g_row, g_col = (iota((128, 128), 0), iota((128, 128), 1))
        values = jnp.where((g_row >> 6) == (g_col >> 6), wide, 0.0)
        g_step = 1.0 / jnp.max(jnp.sum(jnp.abs(values), axis=1, keepdims=True), axis=0, keepdims=True)
        g_eye = jnp.where(g_row == g_col, 1.0, 0.0)
        g_res0 = (g_eye - g_step * values).astype(BF16)
        g_res1 = mm(g_res0, g_res0).astype(BF16)
        gbd[...] = g_step * (g_eye + g_res0.astype(F32) + g_res1.astype(F32) + mm(g_res1, g_res0))

    def selections():
        col = iota((ORDER, cw), 1)
        sel[...] = ones_where((iota((ORDER, cw), 0) == fi * blk + col) & (col < blk))
        q_row, q_col = (iota((blk, n * rpad), 0), iota((blk, n * rpad), 1))
        in_slot = lax.rem(q_col, rpad)
        one = ones_where(((q_col // rpad) * rows + in_slot == q_row) & (in_slot < rows)).astype(F32)
        none = jnp.zeros_like(one)
        squeeze[...] = jnp.concatenate(
            [jnp.concatenate([one, none], axis=1), jnp.concatenate([none, one], axis=1)], axis=0
        ).astype(BF16)

    def relay():
        @pl.when(sec < n_sec - 1)
        def _():
            send_chain().wait_recv()
            top_p[...] = arr[...].astype(F32)

        lane = iota((256, 128), 1)
        grad = jnp.where(pre_p[...] > 0, top_p[...], 0.0)
        gcat[256:512, :] = grad.astype(BF16)
        gcat[0:256, :] = jnp.where(lane == 127, 0.0, pltpu.roll(grad, 127, 1)).astype(BF16)
        gcat[512:768, :] = jnp.where(lane == 0, 0.0, pltpu.roll(grad, 1, 1)).astype(BF16)
        obuf[...] = mm(bw[...], gcat[...]).astype(BF16)

        @pl.when(sec > 0)
        def _():
            send_chain().start()

        full = mm_nt(ash[...], gcat[256:512, :])
        left = iota((64, 128), 1) < 64

        def part(aa, c, y):
            total = None
            for x in range(2):
                x2 = x - (aa - 1)
                if 0 <= x2 < 2:
                    row = 256 * c + 64 * (2 * x + y)
                    term = full[row : row + 64, 128 * x2 : 128 * x2 + 128]
                    total = term if total is None else total + term
            return total

        parts = {(aa, c, y): part(aa, c, y) for aa in range(3) for c in range(3) for y in range(2)}
        for m, (one, two) in enumerate(PAIRED):
            if one[1] == 2:
                tile = jnp.where(left, parts[one[0], one[2], 1], parts[one[0], one[2], 0])
            else:
                first = parts[one[0], one[2], 0] + pltpu.roll(parts[one[0], one[2], 1], 64, 1)
                second = pltpu.roll(parts[two[0], two[2], 0], 64, 1) + parts[two[0], two[2], 1]
                tile = jnp.where(left, first, second)
            at = (64 * m) % frows
            wg[(64 * m) // frows, at : at + 64, :] = tile.astype(wg.dtype)

        if "red" in PARTS:
            def start(k):
                @pl.when(holds(f_peer(k)))
                def _():
                    gr_copy(k, f_peer(k), fi).start()

            each(start)
        og[...] = mm(channel_last(False), obuf[...]).astype(BF16)

    def inverse_a():
        def wait(k, largest):
            slot = f_from(k)
            fa_copy(k, slot, f_peer(k)).wait_recv()
            sums = jnp.sum(jnp.abs(apad[slot].astype(F32)), axis=1, keepdims=True)
            return jnp.maximum(largest, sums)

        own_sums = jnp.sum(jnp.abs(own[...].astype(F32)), axis=1, keepdims=True)
        largest = lax.fori_loop(1, n, wait, own_sums)
        mx[si] = jnp.broadcast_to(jnp.max(largest, axis=0, keepdims=True), (8, 128))
        each(lambda k: sm_copy(k, si, s_peer(k)).start())
        piece[...] = mm(apad[...].reshape(n * rpad, ORDER), sel[...]).astype(BF16).reshape(n, rpad, cw)

        @pl.when(core == 0)
        def _():
            each(lambda k: sa_copy(k, si, s_peer(k), False).start())
            spc[si] = piece[...]

        @pl.when(core == 1)
        def _():
            each(lambda k: sa_copy(k, si, s_peer(k), True).start())
            spc[:, si] = piece[...]

        each(lambda k: sm_copy(k, s_from(k), s_peer(k)).wait_recv())
        stp[...] = 1.0 / jnp.broadcast_to(
            jnp.max(jnp.max(mx[...], axis=0), axis=0, keepdims=True), (8, 128)
        )
        step = stp[0:1, 0:1]
        local = iota((rpad, ORDER), 0)
        from_diag = jnp.where(local < rows, iota((rpad, ORDER), 1) - local, -1)

        def residual_rows(u, carry):
            eye = jnp.where(from_diag == f_dp(u) * rows, 1.0, 0.0)
            rrow[u] = (eye - step * apad[u].astype(F32)).astype(BF16)
            return carry

        lax.fori_loop(0, n, residual_rows, 0)

    def inverse_b():
        @pl.when(core == 0)
        def _():
            each(lambda k: sa_copy(k, s_from(k), s_peer(k), False).wait_recv())

        @pl.when(core == 1)
        def _():
            each(lambda k: sa_copy(k, s_from(k), s_peer(k), True).wait_recv())

        step = stp[0:1, 0:1]
        for m in range(n // 2):
            pair = spc[2 * m : 2 * m + 2].reshape(2 * n * rpad, cw)
            at = slice(2 * blk * m, 2 * blk * m + 2 * blk)
            rcol[at, :] = (sel[at, :].astype(F32) - step * mm(squeeze[...], pair)).astype(BF16)
        square = mm(rrow[...].reshape(n * rpad, ORDER), rcol[...]).astype(BF16)
        partial = mm_nt(square, rcol[...]) + mm_nt(square, sel[...])
        pbuf[...] = partial.astype(BF16).reshape(pbuf.shape)
        each(lambda k: pr_copy(k, f_peer(k), fi).start())

    def inverse_c():
        step = stp[0:1, 0:1]
        own_row = iota((rpad, ORDER), 0)
        eye = jnp.where((iota((rpad, ORDER), 1) - own_row == dp * rows) & (own_row < rows), 1.0, 0.0)
        res = (eye - step * own[...].astype(F32)).astype(BF16).astype(F32)
        xf[:, 0:ORDER] = eye + res + pbuf[fi].astype(F32)

        def add(k, carry):
            slot = f_from(k)
            pr_copy(k, f_peer(k), slot).wait_recv()
            xf[:, 0:ORDER] += prc[slot].astype(F32)
            return carry

        lax.fori_loop(1, n, add, 0)
        xf[:, 0:ORDER] = step * xf[:, 0:ORDER]
        oi[:, 0, :] = xf[0:rows, 0:ORDER]
        xf[:, ORDER:] = jnp.zeros((rpad, xf.shape[1] - ORDER), F32)
        left = iota((rpad, 128), 1) < 64

        def tap_lanes(abc, half):
            tap = tap_of(abc)
            group = xf[:, 128 * (tap // 2) : 128 * (tap // 2) + 128]
            return group if tap % 2 == half else pltpu.roll(group, 64, 1)

        for side in range(2):
            for m in range(TILES // 2):
                one, two = (PAIRED[2 * m][side], PAIRED[2 * m + 1][side])
                tile = jnp.where(left, tap_lanes(one, 0), tap_lanes(two, 1))
                if side == 1 and 2 * m + 1 == TILES - 1:
                    tile = jnp.where(left, tile, 0.0)
                first = tile.astype(BF16)
                row = 2 * side * rpad
                xcat[row : row + rpad, 128 * m : 128 * m + 128] = first
                xcat[row + rpad : row + 2 * rpad, 128 * m : 128 * m + 128] = (
                    tile - first.astype(F32)
                ).astype(BF16)

    def reduce_a():
        total = wg[fi].astype(F32)
        each(lambda k: gr_copy(k, fi, f_from(k)).wait_recv())
        for k in range(1, n):
            total = total + rg[f_from(k)].astype(F32)
        sbuf[...] = total.astype(sbuf.dtype)
        each(lambda k: rr_copy(k, si, s_peer(k)).start())

    def reduce_b():
        total = sbuf[...].astype(F32)
        each(lambda k: rr_copy(k, s_from(k), s_peer(k)).wait_recv())
        for k in range(1, n):
            total = total + rs[s_from(k)].astype(F32)
        pall[fi] = mm(total / (n * n), gbd[...], HIGH).astype(BF16)
        each(lambda k: af_copy(k, fi, f_peer(k)).start())

    def finish():
        def wait(k):
            @pl.when(holds(f_from(k)))
            def _():
                af_copy(k, f_from(k), f_peer(k)).wait_recv()

        each(wait)
        terms = mm(xcat[...], pall[...].reshape(n * frows, 128)[0 : 64 * TILES, :])
        firsts = terms[0:rpad, :] + terms[rpad : 2 * rpad, :]
        seconds = terms[2 * rpad : 3 * rpad, :] + terms[3 * rpad : 4 * rpad, :]
        update = firsts + pltpu.roll(seconds, 64, 1)
        ou[:, 0, :] = update[0:rows, 0:64]

    barrier = pltpu.get_barrier_semaphore()
    each(lambda k: pl.semaphore_signal(barrier, inc=1, device_id=f_dev(f_peer(k)), device_id_type=MESH))
    each(lambda k: pl.semaphore_signal(barrier, inc=1, device_id=s_dev(s_peer(k)), device_id_type=MESH))
    for near in (sec + 1, sec + n_sec - 1):
        pl.semaphore_signal(
            barrier, inc=1, device_id=(lax.rem(near, n_sec), dp), device_id_type=MESH
        )

    for one in inputs:
        one.start()
    inputs[0].wait()
    own[...] = jnp.zeros_like(own)
    own[0:rows, :] = a[...]
    inputs[1].wait()
    conv_matrices()
    for one in inputs[2:]:
        one.wait()
    pre_p[...] = mm(channel_last(True), pre[...])
    top_p[...] = mm(channel_last(True), top[...])
    pl.semaphore_wait(barrier, 2 * n)

    if "inv" in PARTS:
        each(lambda k: fa_copy(k, fi, f_peer(k)).start())
        apad[fi] = own[...]

    lanes = iota((256, 128), 1)
    act_p = mm(channel_last(True), acts[...])
    ash[0:256, :] = jnp.where(lanes == 0, 0.0, pltpu.roll(act_p, 1, 1)).astype(BF16)
    ash[256:512, :] = act_p.astype(BF16)
    ash[512:768, :] = jnp.where(lanes == 127, 0.0, pltpu.roll(act_p, 127, 1)).astype(BF16)
    if wg.shape[0] * frows > 64 * TILES:
        wg[n - 1, frows - (1024 - 64 * TILES) :, :] = jnp.zeros((1024 - 64 * TILES, 128), wg.dtype)

    if "chain" in PARTS:
        pl.when(sec >= early)(relay)
    selections()
    small_inverse()
    if "inv" in PARTS:
        inverse_a()
    if "chain" in PARTS:
        pl.when(sec < early)(relay)
    if "red" in PARTS:
        pl.when(holds(fi))(reduce_a)
    if "inv" in PARTS:
        inverse_b()
    if "red" in PARTS:
        pl.when(holds(fi))(reduce_b)
    if "inv" in PARTS:
        inverse_c()
    if "red" in PARTS:
        finish()

    if "inv" in PARTS:
        each(lambda k: fa_copy(k, fi, f_peer(k)).wait_send())
        each(lambda k: sm_copy(k, si, s_peer(k)).wait_send())

        @pl.when(core == 0)
        def _():
            each(lambda k: sa_copy(k, si, s_peer(k), False).wait_send())

        @pl.when(core == 1)
        def _():
            each(lambda k: sa_copy(k, si, s_peer(k), True).wait_send())

        each(lambda k: pr_copy(k, f_peer(k), fi).wait_send())

    if "red" in PARTS:
        def gr_done(k):
            @pl.when(holds(f_peer(k)))
            def _():
                gr_copy(k, f_peer(k), fi).wait_send()

        each(gr_done)

        @pl.when(holds(fi))
        def _():
            each(lambda k: rr_copy(k, si, s_peer(k)).wait_send())
            each(lambda k: af_copy(k, fi, f_peer(k)).wait_send())

    if "chain" in PARTS:
        @pl.when(sec > 0)
        def _():
            send_chain().wait_send()


def make_call(n_sec, n, early, grad_type=BF16):
    rows = ORDER // (n * n)
    rpad = pad_to(rows, 16)
    blk = rows * n
    cw = pad_to(blk, 128)
    frows = 1024 // n
    cfg = (n_sec, n, rows, rpad, early)
    vmem = pltpu.VMEM
    dma = pltpu.SemaphoreType.DMA
    scratch = [
        vmem((256, 128), BF16),
        vmem((256, 128), BF16),
        vmem((256, 128), BF16),
        vmem((64, ORDER), BF16),
        vmem((rows, ORDER), BF16),
        vmem((64, 64), BF16),
        dma((6,)),
        vmem((ORDER, 128), F32),
        vmem((256, 768), BF16),
        vmem((256, 128), F32),
        vmem((256, 128), F32),
        vmem((768, 128), BF16),
        vmem((256, 128), BF16),
        vmem((256, 128), BF16),
        vmem((768, 128), BF16),
        vmem((rpad, ORDER), BF16),
        vmem((n, rpad, ORDER), BF16),
        vmem((ORDER, cw), BF16),
        vmem((2 * blk, 2 * n * rpad), BF16),
        vmem((n, n, rpad, cw), BF16),
        vmem((n, rpad, cw), BF16),
        vmem((n, 8, 128), F32),
        vmem((n, rpad, ORDER), BF16),
        vmem((ORDER, cw), BF16),
        vmem((n, rpad, ORDER), BF16),
        vmem((n, rpad, ORDER), BF16),
        vmem((rpad, pad_to(ORDER, 128)), F32),
        vmem((4 * rpad, 64 * TILES), BF16),
        vmem((n, frows, 128), grad_type),
        vmem((n, frows, 128), grad_type),
        vmem((frows, 128), grad_type),
        vmem((n, frows, 128), grad_type),
        vmem((n, frows, 128), BF16),
        vmem((128, 128), F32),
        vmem((8, 128), F32),
        dma, dma,
    ]
    scratch += [dma((n - 1,)) for _ in range(14)]
    hbm = pl.BlockSpec(memory_space=pltpu.HBM)
    spec = pl.BlockSpec(memory_space=pltpu.VMEM)
    return pl.pallas_call(
        functools.partial(kernel, cfg),
        out_shape=(
            jax.ShapeDtypeStruct((256, 128), BF16),
            jax.ShapeDtypeStruct((rows, 1, 64), F32),
            jax.ShapeDtypeStruct((rows, 1, ORDER), F32),
        ),
        in_specs=[hbm] * 6,
        out_specs=(spec, spec, spec),
        scratch_shapes=scratch,
        compiler_params=pltpu.CompilerParams(
            collective_id=0, has_side_effects=True, vmem_limit_bytes=VMEM_MIB * 1024 * 1024
        ),
    )


def build(mesh, n, early):
    n_sec = mesh.shape["section"]

    def shards(acts, preacts, top_grad, weights, a_factor, g_factor):
        call = make_call(n_sec, n, early)
        grads, update, inverse = call(
            acts.reshape(256, 128),
            preacts.reshape(256, 128),
            top_grad.reshape(256, 128),
            weights[0],
            a_factor[0],
            g_factor[0],
        )
        return (
            grads.reshape(acts.shape),
            update.transpose(1, 0, 2),
            inverse.transpose(1, 0, 2),
        )

    placed = (
        P("section", "dp", None, None, None, None, None),
        P("section", "dp", None, None, None, None, None),
        P("dp", None, None, None, None, None),
        P("section", None, None),
        P("section", "dp", None),
        P("section", None, None),
    )
    return jax.shard_map(
        shards,
        mesh=mesh,
        in_specs=placed,
        out_specs=(
            P("section", "dp", None, None, None, None, None),
            P("section", "dp", None),
            P("section", "dp", None),
        ),
        check_vma=False,
    )


def solution(mesh):
    return build(mesh, 8, EARLY)
```

```python
import functools

import jax
import jax.numpy as jnp
from jax import lax
from jax.experimental import pallas as pl
from jax.experimental.pallas import tpu as pltpu
from jax.sharding import PartitionSpec as P

MESH = pl.DeviceIdType.MESH
F32 = jnp.float32
BF16 = jnp.bfloat16
HIGH = lax.Precision.HIGHEST

ORDER = 1728
PAIRED = [((a, 2, c), (a, 0, c)) for a in range(3) for c in range(3)]
MIDDLE = [(a, 1, c) for a in range(3) for c in range(3)]
PAIRED += [(MIDDLE[2 * m], MIDDLE[min(2 * m + 1, 8)]) for m in range(5)]
TILES = len(PAIRED)
PARTS = ("inv", "chain", "red")
PASS = 4
LATE_CONV = 0
VMEM_MIB = 56


def tap_of(abc):
    return (abc[0] * 3 + abc[1]) * 3 + abc[2]


def iota(shape, dim):
    return lax.broadcasted_iota(jnp.int32, shape, dim)


def ones_where(mask):
    return jnp.where(mask, 1.0, 0.0).astype(BF16)


def mm(left, right, precision=None):
    return lax.dot_general(
        left, right, (((1,), (0,)), ((), ())), precision=precision, preferred_element_type=F32
    )


def mm_nt(left, right):
    return lax.dot_general(left, right, (((1,), (1,)), ((), ())), preferred_element_type=F32)


def pad_to(value, step):
    return -(-value // step) * step


def kernel(cfg, acts_h, pre_h, top_h, w_h, a_h, gf_h, og, ou, oi, *scratch):
    (
        acts, pre, top, w, a, gf, in_s,
        wt, bw, pre_p, top_p, ash, arr, obuf, gcat, own, apad, squeeze, spc, piece, mx,
        rrow, both, pbuf, prc, xf, xcat, wg, rg, sbuf, rs, pall, gbd, stp,
        ch_s, ch_r, fa_s, fa_r, sa_s, sa_r, sm_s, sm_r, pr_s, pr_r,
        gr_s, gr_r, rr_s, rr_r, af_s, af_r,
    ) = scratch
    n_sec, n, rows, rpad = cfg
    blk = rows * n
    cw = both.shape[1] // 2
    frows = rg.shape[1]
    sec = lax.axis_index("section")
    dp = lax.axis_index("dp")
    core = lax.rem(sec, 2)
    low, high = lax.rem(dp, n), dp // n
    fi = low + core * (high - low)
    si = high + core * (low - high)

    def f_dp(index):
        return si * n + index + core * (n - 1) * (index - si)

    def s_dp(index):
        return index * n + fi + core * (n - 1) * (fi - index)

    ns = n // 2

    def along(index, k, way):
        far = ns + (k // 2) * (2 * lax.rem(k, 2) - 1)
        return lax.rem(index + way * far + n, n)

    def across(index, k, way):
        same = k // (ns + 1)
        plane, x = index // ns, lax.rem(index, ns)
        step = k - 1 - (ns - 1) * same
        return (plane + (1 - same) * (1 - 2 * plane)) * ns + lax.rem(x + way * step + ns, ns)

    def f_near(k, way):
        return along(fi, k, way) + core * (across(fi, k, way) - along(fi, k, way))

    def s_near(k, way):
        return across(si, k, way) + core * (along(si, k, way) - across(si, k, way))

    def f_peer(k):
        return f_near(k, 1)

    def f_from(k):
        return f_near(k, -1)

    def s_peer(k):
        return s_near(k, 1)

    def s_from(k):
        return s_near(k, -1)

    def f_dev(index):
        return (sec, f_dp(index))

    def s_dev(index):
        return (sec, s_dp(index))

    def copy_to(src, dst, ss, rr, k, device):
        return pltpu.make_async_remote_copy(
            src_ref=src, dst_ref=dst, send_sem=ss.at[k - 1], recv_sem=rr.at[k - 1],
            device_id=device, device_id_type=MESH,
        )

    def each(body):
        lax.fori_loop(1, n, lambda k, carry: (body(k), carry)[1], 0)

    def fa_copy(k, slot, index):
        return copy_to(own, apad.at[slot], fa_s, fa_r, k, f_dev(index))

    def fx_copy(k):
        partner = f_from(1)
        plane, x = fi // ns, lax.rem(fi, ns)
        return copy_to(
            apad.at[partner], apad.at[partner], fa_s, fa_r, k,
            f_dev(plane * ns + lax.rem(x + k - 1, ns)),
        )

    def pass_on():
        fa_copy(1, f_from(1), f_peer(1)).wait_recv()
        for k in range(2, ns + 1):
            fx_copy(k).start()

    def sa_copy(k, slot, index, by_column):
        dst = spc.at[:, slot] if by_column else spc.at[slot]
        return copy_to(piece, dst, sa_s, sa_r, k, s_dev(index))

    def sm_copy(k, slot, index):
        return copy_to(mx.at[si], mx.at[slot], sm_s, sm_r, k, s_dev(index))

    def pr_copy(k, chunk, slot):
        return copy_to(pbuf.at[chunk], prc.at[slot], pr_s, pr_r, k, f_dev(chunk))

    def gr_copy(k, chunk, slot):
        return copy_to(wg.at[chunk], rg.at[slot], gr_s, gr_r, k, f_dev(chunk))

    def rr_copy(k, slot, index):
        return copy_to(sbuf, rs.at[slot], rr_s, rr_r, k, s_dev(index))

    def af_copy(k, slot, index):
        return copy_to(pall.at[fi], pall.at[slot], af_s, af_r, k, f_dev(index))

    def send_chain():
        return pltpu.make_async_remote_copy(
            src_ref=obuf, dst_ref=arr, send_sem=ch_s, recv_sem=ch_r,
            device_id=(lax.rem(sec - 1 + n_sec, n_sec), dp), device_id_type=MESH,
        )

    def holds(chunk):
        return chunk * frows < TILES * 64

    inputs = [
        pltpu.make_async_copy(src, dst, in_s.at[m])
        for m, (src, dst) in enumerate(
            [(a_h, a), (w_h, w), (pre_h, pre), (top_h, top), (acts_h, acts), (gf_h, gf)]
        )
    ]

    def conv_matrices():
        wpair = jnp.concatenate([w[...], w[...]], axis=0).astype(F32)
        for m in range(ORDER // 128):
            wt[128 * m : 128 * m + 128, :] = wpair[:, 128 * m : 128 * m + 128].T
        last = 128 * (ORDER // 128)
        wt[last:ORDER, :] = wpair[:, last:ORDER].T
        left64 = iota((64, 128), 1) < 64

        def wtap(aa, b, c):
            start = 64 * tap_of((aa, b, c))
            return wt[start : start + 64, :]

        for c in range(3):
            for x in range(2):
                for y in range(2):
                    for x2 in range(2):
                        block = jnp.where(left64, wtap(x - x2 + 1, y + 1, c), wtap(x - x2 + 1, y, c))
                        row = 64 * (2 * x + y)
                        lane = 256 * c + 128 * x2
                        bw[row : row + 64, lane : lane + 128] = block.astype(BF16)

    def channel_last(forward):
        one, two = (iota((256, 256), 0), iota((256, 256), 1))
        if not forward:
            one, two = two, one
        return ones_where(two == (one & 63) * 4 + (one >> 6))

    def small_inverse():
        dup = ones_where(iota((64, 128), 0) == (iota((64, 128), 1) & 63))
        dup_t = ones_where(iota((128, 64), 1) == (iota((128, 64), 0) & 63))
        wide = mm(mm(dup_t, gf[...]).astype(BF16), dup)
        g_row, g_col = (iota((128, 128), 0), iota((128, 128), 1))
        values = jnp.where((g_row >> 6) == (g_col >> 6), wide, 0.0)
        g_step = 1.0 / jnp.max(jnp.sum(jnp.abs(values), axis=1, keepdims=True), axis=0, keepdims=True)
        g_eye = jnp.where(g_row == g_col, 1.0, 0.0)
        g_res0 = (g_eye - g_step * values).astype(BF16)
        g_res1 = mm(g_res0, g_res0).astype(BF16)
        gbd[...] = g_step * (g_eye + g_res0.astype(F32) + g_res1.astype(F32) + mm(g_res1, g_res0))

    def selections():
        col = iota((ORDER, cw), 1)
        both[:, cw:] = ones_where((iota((ORDER, cw), 0) == fi * blk + col) & (col < blk))
        q_row, q_col = (iota((blk, n * rpad), 0), iota((blk, n * rpad), 1))
        in_slot = lax.rem(q_col, rpad)
        one = ones_where(((q_col // rpad) * rows + in_slot == q_row) & (in_slot < rows)).astype(F32)
        none = jnp.zeros_like(one)
        squeeze[...] = jnp.concatenate(
            [jnp.concatenate([one, none], axis=1), jnp.concatenate([none, one], axis=1)], axis=0
        ).astype(BF16)

    def relay():
        @pl.when(sec < n_sec - 1)
        def _():
            send_chain().wait_recv()
            top_p[...] = arr[...].astype(F32)

        lane = iota((256, 128), 1)
        grad = jnp.where(pre_p[...] > 0, top_p[...], 0.0)
        gcat[256:512, :] = grad.astype(BF16)
        gcat[0:256, :] = jnp.where(lane == 127, 0.0, pltpu.roll(grad, 127, 1)).astype(BF16)
        gcat[512:768, :] = jnp.where(lane == 0, 0.0, pltpu.roll(grad, 1, 1)).astype(BF16)
        obuf[...] = mm(bw[...], gcat[...]).astype(BF16)

        @pl.when(sec > 0)
        def _():
            send_chain().start()

        full = mm_nt(ash[...], gcat[256:512, :])
        left = iota((64, 128), 1) < 64

        def part(aa, c, y):
            total = None
            for x in range(2):
                x2 = x - (aa - 1)
                if 0 <= x2 < 2:
                    row = 256 * c + 64 * (2 * x + y)
                    term = full[row : row + 64, 128 * x2 : 128 * x2 + 128]
                    total = term if total is None else total + term
            return total

        parts = {(aa, c, y): part(aa, c, y) for aa in range(3) for c in range(3) for y in range(2)}
        for m, (one, two) in enumerate(PAIRED):
            if one[1] == 2:
                tile = jnp.where(left, parts[one[0], one[2], 1], parts[one[0], one[2], 0])
            else:
                first = parts[one[0], one[2], 0] + pltpu.roll(parts[one[0], one[2], 1], 64, 1)
                second = pltpu.roll(parts[two[0], two[2], 0], 64, 1) + parts[two[0], two[2], 1]
                tile = jnp.where(left, first, second)
            at = (64 * m) % frows
            wg[(64 * m) // frows, at : at + 64, :] = tile.astype(wg.dtype)

        if "red" in PARTS:
            def start(k):
                @pl.when(holds(f_peer(k)))
                def _():
                    gr_copy(k, f_peer(k), fi).start()

            each(start)
        og[...] = mm(channel_last(False), obuf[...]).astype(BF16)

    def inverse_a():
        def wait(k, largest):
            slot = f_from(k)

            @pl.when((core == 0) | (k > 1))
            def _():
                fa_copy(k, slot, f_peer(k)).wait_recv()

            sums = jnp.sum(jnp.abs(apad[slot].astype(F32)), axis=1, keepdims=True)
            return jnp.maximum(largest, sums)

        own_sums = jnp.sum(jnp.abs(own[...].astype(F32)), axis=1, keepdims=True)
        largest = lax.fori_loop(1, n, wait, own_sums)
        mx[si] = jnp.broadcast_to(jnp.max(largest, axis=0, keepdims=True), (8, 128))
        each(lambda k: sm_copy(k, si, s_peer(k)).start())
        piece[...] = mm(apad[...].reshape(n * rpad, ORDER), both[:, cw:]).astype(BF16).reshape(n, rpad, cw)

        @pl.when(core == 0)
        def _():
            each(lambda k: sa_copy(k, si, s_peer(k), False).start())
            spc[si] = piece[...]

        @pl.when(core == 1)
        def _():
            each(lambda k: sa_copy(k, si, s_peer(k), True).start())
            spc[:, si] = piece[...]

        each(lambda k: sm_copy(k, s_from(k), s_peer(k)).wait_recv())
        stp[...] = 1.0 / jnp.broadcast_to(
            jnp.max(jnp.max(mx[...], axis=0), axis=0, keepdims=True), (8, 128)
        )
        step = stp[0:1, 0:1]
        local = iota((rpad, ORDER), 0)
        from_diag = jnp.where(local < rows, iota((rpad, ORDER), 1) - local, -1)

        def residual_rows(u, carry):
            eye = jnp.where(from_diag == f_dp(u) * rows, 1.0, 0.0)
            rrow[u] = (eye - step * apad[u].astype(F32)).astype(BF16)
            return carry

        lax.fori_loop(0, n, residual_rows, 0)

    def inverse_b():
        @pl.when(core == 0)
        def _():
            each(lambda k: sa_copy(k, s_from(k), s_peer(k), False).wait_recv())

        @pl.when(core == 1)
        def _():
            each(lambda k: sa_copy(k, s_from(k), s_peer(k), True).wait_recv())

        step = stp[0:1, 0:1]
        for m in range(n // 2):
            pair = spc[2 * m : 2 * m + 2].reshape(2 * n * rpad, cw)
            at = slice(2 * blk * m, 2 * blk * m + 2 * blk)
            both[at, 0:cw] = (both[at, cw:].astype(F32) - step * mm(squeeze[...], pair)).astype(BF16)
        square = mm(rrow[...].reshape(n * rpad, ORDER), both[:, 0:cw]).astype(BF16)
        partial = mm_nt(jnp.concatenate([square, square], axis=1), both[...])
        pbuf[...] = partial.astype(BF16).reshape(pbuf.shape)
        each(lambda k: pr_copy(k, f_peer(k), fi).start())

    def inverse_c():
        step = stp[0:1, 0:1]
        own_row = iota((rpad, ORDER), 0)
        eye = jnp.where((iota((rpad, ORDER), 1) - own_row == dp * rows) & (own_row < rows), 1.0, 0.0)
        res = (eye - step * own[...].astype(F32)).astype(BF16).astype(F32)
        xf[:, 0:ORDER] = eye + res + pbuf[fi].astype(F32)

        def add(k, carry):
            slot = f_from(k)
            pr_copy(k, f_peer(k), slot).wait_recv()
            xf[:, 0:ORDER] += prc[slot].astype(F32)
            return carry

        lax.fori_loop(1, n, add, 0)
        xf[:, 0:ORDER] = step * xf[:, 0:ORDER]
        oi[:, 0, :] = xf[0:rows, 0:ORDER]
        xf[:, ORDER:] = jnp.zeros((rpad, xf.shape[1] - ORDER), F32)
        left = iota((rpad, 128), 1) < 64

        def tap_lanes(abc, half):
            tap = tap_of(abc)
            group = xf[:, 128 * (tap // 2) : 128 * (tap // 2) + 128]
            return group if tap % 2 == half else pltpu.roll(group, 64, 1)

        for side in range(2):
            for m in range(TILES // 2):
                one, two = (PAIRED[2 * m][side], PAIRED[2 * m + 1][side])
                tile = jnp.where(left, tap_lanes(one, 0), tap_lanes(two, 1))
                if side == 1 and 2 * m + 1 == TILES - 1:
                    tile = jnp.where(left, tile, 0.0)
                first = tile.astype(BF16)
                row = 2 * side * rpad
                xcat[row : row + rpad, 128 * m : 128 * m + 128] = first
                xcat[row + rpad : row + 2 * rpad, 128 * m : 128 * m + 128] = (
                    tile - first.astype(F32)
                ).astype(BF16)

    def reduce_a():
        total = wg[fi].astype(F32)
        each(lambda k: gr_copy(k, fi, f_from(k)).wait_recv())
        for k in range(1, n):
            total = total + rg[f_from(k)].astype(F32)
        sbuf[...] = total.astype(sbuf.dtype)
        each(lambda k: rr_copy(k, si, s_peer(k)).start())

    def reduce_b():
        total = sbuf[...].astype(F32)
        each(lambda k: rr_copy(k, s_from(k), s_peer(k)).wait_recv())
        for k in range(1, n):
            total = total + rs[s_from(k)].astype(F32)
        pall[fi] = mm(total / (n * n), gbd[...], HIGH).astype(BF16)
        each(lambda k: af_copy(k, fi, f_peer(k)).start())

    def finish():
        def wait(k):
            @pl.when(holds(f_from(k)))
            def _():
                af_copy(k, f_from(k), f_peer(k)).wait_recv()

        each(wait)
        terms = mm(xcat[...], pall[...].reshape(n * frows, 128)[0 : 64 * TILES, :])
        firsts = terms[0:rpad, :] + terms[rpad : 2 * rpad, :]
        seconds = terms[2 * rpad : 3 * rpad, :] + terms[3 * rpad : 4 * rpad, :]
        update = firsts + pltpu.roll(seconds, 64, 1)
        ou[:, 0, :] = update[0:rows, 0:64]

    barrier = pltpu.get_barrier_semaphore()
    each(lambda k: pl.semaphore_signal(barrier, inc=1, device_id=f_dev(f_peer(k)), device_id_type=MESH))
    each(lambda k: pl.semaphore_signal(barrier, inc=1, device_id=s_dev(s_peer(k)), device_id_type=MESH))
    for near in (sec + 1, sec + n_sec - 1):
        pl.semaphore_signal(
            barrier, inc=1, device_id=(lax.rem(near, n_sec), dp), device_id_type=MESH
        )

    for one in inputs:
        one.start()
    inputs[0].wait()
    own[...] = jnp.zeros_like(own)
    own[0:rows, :] = a[...]
    def prologue():
        inputs[1].wait()
        conv_matrices()
        for one in inputs[2:]:
            one.wait()
        pre_p[...] = mm(channel_last(True), pre[...])
        top_p[...] = mm(channel_last(True), top[...])

    if not LATE_CONV:
        prologue()
    pl.semaphore_wait(barrier, 2 * n)

    if "inv" in PARTS:
        @pl.when(core == 0)
        def _():
            each(lambda k: fa_copy(k, fi, f_peer(k)).start())

        @pl.when(core == 1)
        def _():
            for k in range(1, n):
                if k == 1 or k > ns:
                    fa_copy(k, fi, f_peer(k)).start()

        apad[fi] = own[...]
    if LATE_CONV:
        prologue()

    lanes = iota((256, 128), 1)
    act_p = mm(channel_last(True), acts[...])
    ash[0:256, :] = jnp.where(lanes == 0, 0.0, pltpu.roll(act_p, 1, 1)).astype(BF16)
    ash[256:512, :] = act_p.astype(BF16)
    ash[512:768, :] = jnp.where(lanes == 127, 0.0, pltpu.roll(act_p, 127, 1)).astype(BF16)
    if wg.shape[0] * frows > 64 * TILES:
        wg[n - 1, frows - (1024 - 64 * TILES) :, :] = jnp.zeros((1024 - 64 * TILES, 128), wg.dtype)

    if "inv" in PARTS:
        pl.when((core == 1) & (sec < PASS))(pass_on)
    if "chain" in PARTS:
        relay()
    if "inv" in PARTS:
        pl.when((core == 1) & (sec >= PASS))(pass_on)
    selections()
    small_inverse()
    if "inv" in PARTS:
        inverse_a()
    if "red" in PARTS:
        pl.when(holds(fi))(reduce_a)
    if "inv" in PARTS:
        inverse_b()
    if "red" in PARTS:
        pl.when(holds(fi))(reduce_b)
    if "inv" in PARTS:
        inverse_c()
    if "red" in PARTS:
        finish()

    if "inv" in PARTS:
        @pl.when(core == 0)
        def _():
            each(lambda k: fa_copy(k, fi, f_peer(k)).wait_send())

        @pl.when(core == 1)
        def _():
            for k in range(1, n):
                (fx_copy(k) if 1 < k <= ns else fa_copy(k, fi, f_peer(k))).wait_send()

        each(lambda k: sm_copy(k, si, s_peer(k)).wait_send())

        @pl.when(core == 0)
        def _():
            each(lambda k: sa_copy(k, si, s_peer(k), False).wait_send())

        @pl.when(core == 1)
        def _():
            each(lambda k: sa_copy(k, si, s_peer(k), True).wait_send())

        each(lambda k: pr_copy(k, f_peer(k), fi).wait_send())

    if "red" in PARTS:
        def gr_done(k):
            @pl.when(holds(f_peer(k)))
            def _():
                gr_copy(k, f_peer(k), fi).wait_send()

        each(gr_done)

        @pl.when(holds(fi))
        def _():
            each(lambda k: rr_copy(k, si, s_peer(k)).wait_send())
            each(lambda k: af_copy(k, fi, f_peer(k)).wait_send())

    if "chain" in PARTS:
        @pl.when(sec > 0)
        def _():
            send_chain().wait_send()


def make_call(n_sec, n, grad_type=BF16):
    rows = ORDER // (n * n)
    rpad = pad_to(rows, 16)
    blk = rows * n
    cw = pad_to(blk, 128)
    frows = 1024 // n
    cfg = (n_sec, n, rows, rpad)
    vmem = pltpu.VMEM
    dma = pltpu.SemaphoreType.DMA
    scratch = [
        vmem((256, 128), BF16),
        vmem((256, 128), BF16),
        vmem((256, 128), BF16),
        vmem((64, ORDER), BF16),
        vmem((rows, ORDER), BF16),
        vmem((64, 64), BF16),
        dma((6,)),
        vmem((ORDER, 128), F32),
        vmem((256, 768), BF16),
        vmem((256, 128), F32),
        vmem((256, 128), F32),
        vmem((768, 128), BF16),
        vmem((256, 128), BF16),
        vmem((256, 128), BF16),
        vmem((768, 128), BF16),
        vmem((rpad, ORDER), BF16),
        vmem((n, rpad, ORDER), BF16),
        vmem((2 * blk, 2 * n * rpad), BF16),
        vmem((n, n, rpad, cw), BF16),
        vmem((n, rpad, cw), BF16),
        vmem((n, 8, 128), F32),
        vmem((n, rpad, ORDER), BF16),
        vmem((ORDER, 2 * cw), BF16),
        vmem((n, rpad, ORDER), BF16),
        vmem((n, rpad, ORDER), BF16),
        vmem((rpad, pad_to(ORDER, 128)), F32),
        vmem((4 * rpad, 64 * TILES), BF16),
        vmem((n, frows, 128), grad_type),
        vmem((n, frows, 128), grad_type),
        vmem((frows, 128), grad_type),
        vmem((n, frows, 128), grad_type),
        vmem((n, frows, 128), BF16),
        vmem((128, 128), F32),
        vmem((8, 128), F32),
        dma, dma,
    ]
    scratch += [dma((n - 1,)) for _ in range(14)]
    hbm = pl.BlockSpec(memory_space=pltpu.HBM)
    spec = pl.BlockSpec(memory_space=pltpu.VMEM)
    return pl.pallas_call(
        functools.partial(kernel, cfg),
        out_shape=(
            jax.ShapeDtypeStruct((256, 128), BF16),
            jax.ShapeDtypeStruct((rows, 1, 64), F32),
            jax.ShapeDtypeStruct((rows, 1, ORDER), F32),
        ),
        in_specs=[hbm] * 6,
        out_specs=(spec, spec, spec),
        scratch_shapes=scratch,
        compiler_params=pltpu.CompilerParams(
            collective_id=0, has_side_effects=True, vmem_limit_bytes=VMEM_MIB * 1024 * 1024
        ),
    )


def build(mesh, n):
    n_sec = mesh.shape["section"]

    def shards(acts, preacts, top_grad, weights, a_factor, g_factor):
        call = make_call(n_sec, n)
        grads, update, inverse = call(
            acts.reshape(256, 128),
            preacts.reshape(256, 128),
            top_grad.reshape(256, 128),
            weights[0],
            a_factor[0],
            g_factor[0],
        )
        return (
            grads.reshape(acts.shape),
            update.transpose(1, 0, 2),
            inverse.transpose(1, 0, 2),
        )

    placed = (
        P("section", "dp", None, None, None, None, None),
        P("section", "dp", None, None, None, None, None),
        P("dp", None, None, None, None, None),
        P("section", None, None),
        P("section", "dp", None),
        P("section", None, None),
    )
    return jax.shard_map(
        shards,
        mesh=mesh,
        in_specs=placed,
        out_specs=(
            P("section", "dp", None, None, None, None, None),
            P("section", "dp", None),
            P("section", "dp", None),
        ),
        check_vma=False,
    )


def solution(mesh):
    return build(mesh, 8)
```
